256 devices in a mesh: expert: 64 (over y, z, core), tensor: 4 (over x).
Axes of the slice: x: 4, y: 4, z: 8, core: 2. Of those that a mesh axis runs over, the one named last changes fastest.
Arguments:
- tokens: bfloat16 [8192, 2048], P('expert', 'tensor'), may hold values from -6 to 6
- routes: int32 [8192, 6], P('expert'), may hold values from 0 to 63, all different within a row; in each aligned block of 128 rows (0 to 127, 128 to 255, ...) at most 24 rows name the same one
- route_weights: float32 [8192, 6], P('expert'), may hold values from 0.1 to 1
- w_gate: bfloat16 [64, 2048, 1408], P('expert', None, 'tensor'), may hold values from -0.125 to 0.125
- w_up: bfloat16 [64, 2048, 1408], P('expert', None, 'tensor'), may hold values from -0.125 to 0.125
- w_down: bfloat16 [64, 1408, 2048], P('expert', 'tensor'), may hold values from -0.15625 to 0.15625
Outputs:
- expert_mix: bfloat16 [8192, 2048], P('expert', 'tensor')
The draws below stay inside these ranges and needn't reach their ends.
Inputs may be any that keep to these rules, and one draw needn't show every extreme that they name: `routes`: each token names 6 different experts; among the 128 tokens of one index of expert (aligned blocks of rows) no expert is named more than 24 times, and in some block some expert exactly 24 times.
All inputs are finite; a program needn't handle non-finite values.
Results may differ from the reference program's by a relative error of at most 0.018.
Values may be sent and summed in bfloat16 or wider, within the bound.
No kernel may reach another device: no remote copies, remote signals or barrier semaphores. Data moves between devices by JAX's collectives and lax.ppermute only.
A program may use at most 64 MiB of HBM per device.

```python
import math
import jax
import jax.numpy as jnp
import numpy as np
from jax import lax

D = 2048
FF = 1408
TOP = 6
TOK_DEV = 128
EXPERTS = 64
TOKENS = 8192
CAP = 24


def block_scale(own_key, extent, cuts, least, largest):
    loudness = 1.0
    for position, blocks in cuts:
        heights = jax.random.uniform(jax.random.fold_in(jax.random.fold_in(own_key, 6), position), (blocks,), jnp.float32, least / len(cuts), largest / len(cuts))
        loudness = loudness * jnp.repeat(jnp.exp(heights), extent[position] // blocks).reshape((-1,) + (1,) * (len(extent) - 1 - position))
    return loudness


def assign_block(key, own, number, rows, number_of, top, bound, slope):
    sequence = jax.random.permutation(key, number_of)
    crowded, usual = load_shares(number_of, rows * top, bound, slope, True), load_shares(number_of, rows * top, bound, slope, False)
    places = jnp.arange(number_of)

    def named(lengths, offset_by):
        used = int((lengths > 0).sum())
        fixed = max(1, used // 4)
        shifted = fixed + (places - fixed + offset_by * (used - fixed)) % max(1, number_of - fixed)
        return jnp.zeros((number_of,), jnp.int32).at[sequence[jnp.where(places < fixed, places, shifted)]].set(jnp.asarray(lengths, jnp.int32))

    lengths = jnp.where(number % 4 == 0, named(crowded, number // 4), named(usual, number - number // 4 - 1))
    mixed = jax.random.permutation(jax.random.fold_in(own, 3), number_of)
    donor, receiver = mixed[0:number_of // 2 * 2:2], mixed[1:number_of // 2 * 2:2]
    margin = jnp.minimum(lengths[donor] - 1, bound - lengths[receiver]) // 2
    margin = jnp.where((donor == sequence[0]) | (receiver == sequence[0]) | (lengths[receiver] == 0), 0, jnp.maximum(margin, 0))
    shifted = jax.random.randint(jax.random.fold_in(own, 4), (number_of // 2,), 0, 1 << 20) % (margin + 1)
    lengths = lengths.at[donor].add(-shifted).at[receiver].add(shifted)
    members = jnp.searchsorted(jnp.cumsum(lengths), jnp.arange(rows * top), side="right").astype(jnp.int32)
    table = members.reshape(top, rows).T
    table = table[jax.random.permutation(jax.random.fold_in(own, 1), rows)]
    offset_by = jax.random.randint(jax.random.fold_in(own, 2), (rows, 1), 0, top)
    return jnp.take_along_axis(table, (jnp.arange(top)[None, :] + offset_by) % top, axis=1)


def load_shares(count, total, reach, slope, full):
    weights = [(1 << 20) // math.isqrt(grade ** slope) + 1 for grade in range(1, count + 1)]
    largest = reach if full else min(reach, max(-(-total // count), total * weights[0] // sum(weights)))
    least = 1 if total - largest >= count - 1 else 0
    counts, rest = [largest] + [least] * (count - 1), total - largest - least * (count - 1)
    while rest > 0:
        movable = [i for i in range(1, count) if counts[i] < largest] or [i for i in range(1, count) if counts[i] < reach]
        mass, left = sum([weights[i] for i in movable]), rest
        for i in movable:
            addition = min(reach - counts[i], max(1, left * weights[i] // mass), rest)
            counts[i] = counts[i] + addition
            rest = rest - addition
    return np.array(counts)


def centred(rng, dims, spread, reach, cuts=(), held_as=jnp.bfloat16):
    loudness = block_scale(rng, dims, cuts, -0.22, 0.18) if cuts else 1.0
    array = jax.random.normal(rng, dims, jnp.float32) * spread * loudness
    return jnp.minimum(jnp.maximum(array, -reach), reach).astype(held_as)


def setup_inputs(seed: int = 0) -> dict:
    key_of = jax.random.split(jax.random.key(seed), 7)
    tokens = centred(key_of[0], (TOKENS, D), 1.0, 6.0, ((0, 64), (1, 4)))
    routes_keys = jax.random.split(jax.random.fold_in(key_of[1], 1), TOKENS // TOK_DEV)
    routes_turns = jax.random.permutation(jax.random.fold_in(key_of[1], 3), TOKENS // TOK_DEV)
    routes = jax.vmap(lambda own, number: assign_block(jax.random.fold_in(key_of[1], 2), own, number, TOK_DEV, EXPERTS, TOP, CAP, 2))(routes_keys, routes_turns).reshape((TOKENS, TOP))
    route_weights = jnp.clip(jnp.exp(math.log(1.0) - 2.3025851 * jax.random.uniform(key_of[2], (TOKENS, TOP), jnp.float32) ** block_scale(key_of[2], (TOKENS, TOP), ((0, 64),), -0.2, 0.2)), 0.1, 1.0)
    w_gate = centred(key_of[3], (EXPERTS, D, FF), D ** -0.5, 0.125, ((0, 64), (2, 4)))
    w_up = centred(key_of[4], (EXPERTS, D, FF), D ** -0.5, 0.125, ((0, 64), (2, 4)))
    w_down = centred(key_of[5], (EXPERTS, FF, D), FF ** -0.5, 0.15625, ((0, 64), (1, 4)))
    return dict(tokens=tokens, routes=routes, route_weights=route_weights, w_gate=w_gate, w_up=w_up, w_down=w_down)


def expert_rows(slot_rows, gate_w, up_w, down_w):
    gate_sum = jnp.dot(slot_rows, gate_w, preferred_element_type=jnp.float32)
    up_sum = jnp.dot(slot_rows, up_w, preferred_element_type=jnp.float32)
    hidden = (jax.nn.silu(gate_sum) * up_sum).astype(jnp.bfloat16)
    return jnp.dot(hidden, down_w, preferred_element_type=jnp.float32).astype(jnp.bfloat16)


def reference(tokens, routes, route_weights, w_gate, w_up, w_down):
    blocks = TOKENS // TOK_DEV
    flat_routes = routes.reshape(blocks, TOK_DEV * TOP)
    onehot = (flat_routes[:, :, None] == jnp.arange(EXPERTS, dtype=jnp.int32)[None, None, :]).astype(jnp.int32)
    slot_rank = jnp.sum((jnp.cumsum(onehot, axis=1) - 1) * onehot, axis=2)
    block_ids = jnp.arange(blocks, dtype=jnp.int32)[:, None]
    target = (flat_routes * (blocks * CAP) + block_ids * CAP + slot_rank).reshape(-1).astype(jnp.int32)
    token_ids = jnp.repeat(jnp.arange(TOKENS, dtype=jnp.int32), TOP)
    slot_token = jnp.full((EXPERTS * blocks * CAP,), TOKENS, jnp.int32).at[target].set(token_ids)
    slot_weight = jnp.zeros((EXPERTS * blocks * CAP,), jnp.float32).at[target].set(route_weights.reshape(-1))
    slot_token = slot_token.reshape(EXPERTS, blocks * CAP)
    slot_weight = slot_weight.reshape(EXPERTS, blocks * CAP)
    padded = jnp.concatenate([tokens, jnp.zeros((1, D), tokens.dtype)], axis=0)

    def visit(totals, inputs):
        ids, weights, gate_w, up_w, down_w = inputs
        outputs = expert_rows(padded[ids], gate_w, up_w, down_w)
        totals = totals.at[ids].add(weights[:, None] * outputs.astype(jnp.float32), mode="drop")
        return totals, None

    totals, _ = lax.scan(visit, jnp.zeros((TOKENS, D), jnp.float32), (slot_token, slot_weight, w_gate, w_up, w_down))
    return totals.astype(jnp.bfloat16)
```

```python
import functools

import jax
import jax.numpy as jnp
import numpy as np
from jax import lax
from jax.experimental import pallas as pl
from jax.experimental.pallas import tpu as pltpu
from jax.sharding import Mesh
from jax.sharding import PartitionSpec as P

CAP = 24
SLOTS = 8
VMEM = pl.BlockSpec(memory_space=pltpu.VMEM)
SMEM = pl.BlockSpec(memory_space=pltpu.SMEM)
LIMIT = 20 * 1024 * 1024


def call(kernel, outs, flops=0, moved=0):
    scalars = [SMEM]

    def run(*args):
        return pl.pallas_call(
            kernel,
            out_shape=outs,
            in_specs=scalars + [VMEM] * (len(args) - 1),
            out_specs=jax.tree.map(lambda _: VMEM, outs),
            compiler_params=pltpu.CompilerParams(vmem_limit_bytes=LIMIT),
            cost_estimate=pl.CostEstimate(flops=flops, bytes_accessed=moved, transcendentals=0),
        )(*args)

    return run


def ranked(x_ref, routes_ref, lanes, step, weights_ref=None):
    tokens = routes_ref.shape[1]
    swap = x_ref[0] // 2
    rows = lax.broadcasted_iota(jnp.int32, (lanes, tokens), 0)
    named, slot = (rows // SLOTS) * step, rows % SLOTS
    routes = routes_ref[...] ^ swap
    member = jnp.zeros((lanes, tokens), jnp.float32)
    weight = jnp.zeros((lanes, tokens), jnp.float32)
    for k in range(routes.shape[0]):
        hit = routes[k : k + 1, :] == named
        member = jnp.where(hit, 1.0, member)
        if weights_ref is not None:
            weight = jnp.where(hit, weights_ref[k : k + 1, :], weight)
    earlier = lax.broadcasted_iota(jnp.int32, (tokens, tokens), 0)
    later = lax.broadcasted_iota(jnp.int32, (tokens, tokens), 1)
    before = jnp.where(earlier < later, 1.0, 0.0).astype(jnp.bfloat16)
    rank = jnp.dot(member.astype(jnp.bfloat16), before, preferred_element_type=jnp.float32)
    return jnp.where(member > 0.0, rank, -1.0), slot, weight


def pick_kernel(x_ref, routes_ref, tokens_ref, *outs):
    rank, slot, _ = ranked(x_ref, routes_ref, outs[0].shape[0], 1)
    tokens = tokens_ref[...]
    for chunk, out in enumerate(outs):
        pick = jnp.where(rank == (slot + chunk * SLOTS).astype(jnp.float32), 1.0, 0.0).astype(jnp.bfloat16)
        out[...] = jnp.dot(pick, tokens, preferred_element_type=jnp.float32).astype(jnp.bfloat16)


def weigh_kernel(x_ref, routes_ref, weights_ref, *outs):
    rank, slot, weight = ranked(x_ref, routes_ref, outs[0].shape[0], 2, weights_ref)
    for chunk, out in enumerate(outs):
        out[...] = jnp.where(rank == (slot + chunk * SLOTS).astype(jnp.float32), weight, 0.0)


def columns_kernel(x_ref, down_ref, mine_ref, theirs_ref):
    x = x_ref[0]
    quarter = mine_ref.shape[1] // 2

    def part(q):
        return down_ref[:, pl.ds(pl.multiple_of(q * quarter, quarter), quarter)]

    mine_ref[:, :quarter] = part(x)
    mine_ref[:, quarter:] = part(x ^ 3)
    theirs_ref[:, :quarter] = part(x ^ 1)
    theirs_ref[:, quarter:] = part(x ^ 2)


def along(value, weight):
    return lax.dot_general(value, weight, (((1,), (1,)), ((), ())), preferred_element_type=jnp.float32)


def hidden_kernel(x_ref, own, near, far, across, gate0, up0, gate1, up1, out):
    x = x_ref[0]
    quarter = own.shape[1]
    pieces = [(own, x), (near, x ^ 1), (far, x ^ 3), (across, x ^ 2)]
    for half, (gate_ref, up_ref) in enumerate(((gate0, up0), (gate1, up1))):
        gate, up = 0.0, 0.0
        for ref, q in pieces:
            span = pl.ds(pl.multiple_of(q * quarter, quarter), quarter)
            value = ref[...]
            gate = gate + along(value, gate_ref[:, span])
            up = up + along(value, up_ref[:, span])
        out[half] = (gate / (1.0 + jnp.exp(-gate)) * up).astype(jnp.bfloat16)


def down_kernel(x_ref, here, there, down0, down1, down2, down3, out):
    total = jnp.dot(here[0], down0[...], preferred_element_type=jnp.float32)
    total = total + jnp.dot(here[1], down1[...], preferred_element_type=jnp.float32)
    total = total + jnp.dot(there[0], down2[...], preferred_element_type=jnp.float32)
    total = total + jnp.dot(there[1], down3[...], preferred_element_type=jnp.float32)
    out[...] = total.astype(jnp.bfloat16)


def across_rows(weight, value):
    return lax.dot_general(weight, value, (((0,), (0,)), ((), ())), preferred_element_type=jnp.float32)


def mixed(weight, value):
    high = weight.astype(jnp.bfloat16)
    low = (weight - high.astype(jnp.float32)).astype(jnp.bfloat16)
    return across_rows(high, value) + across_rows(low, value)


def mix_first_kernel(x_ref, weight, value, out):
    out[...] = mixed(weight[...], value[...])


def mix_kernel(x_ref, total, weight, value, out):
    out[...] = total[...] + mixed(weight[...], value[...])


def mix_last_kernel(x_ref, total, weight, value, keep, send):
    half = keep.shape[1]
    done = total[...] + mixed(weight[...], value[...])
    keep[...] = done[:, :half]
    send[...] = done[:, half:].astype(jnp.bfloat16)


def move_x(value, flip):
    return lax.ppermute(value, "x", [(i, i ^ flip) for i in range(4)])


def move_core(value):
    return lax.ppermute(value, "c", [(0, 1), (1, 0)])


def to_group(value):
    pairs = []
    for x in range(4):
        for core in range(2):
            stays = (x // 2) == core
            target = (x, 1 - core) if stays else (x ^ 3, core)
            pairs.append((core * 4 + x, target[1] * 4 + target[0]))
    return lax.ppermute(value, ("c", "x"), pairs)


def shards(tokens, routes, route_weights, w_gate, w_up, w_down):
    rows, quarter = tokens.shape
    half_ff = w_gate.shape[2]
    routes, route_weights = routes.T, route_weights.T
    w_gate, w_up = jnp.swapaxes(w_gate, 1, 2), jnp.swapaxes(w_up, 1, 2)
    chips = 32
    chunks = CAP // SLOTS
    at = chips * SLOTS
    me = lax.axis_index("x").astype(jnp.int32).reshape(1)
    bf16, f32 = jnp.bfloat16, jnp.float32

    def shape(*dims, dtype=bf16):
        return jax.ShapeDtypeStruct(dims, dtype)

    outgoing = call(pick_kernel, [shape(2 * at, quarter)] * chunks)(me, routes, tokens)
    mixing = call(weigh_kernel, [shape(at, rows, dtype=f32)] * chunks)(me, routes, route_weights)

    gate0, up0 = to_group(w_gate[0]), to_group(w_up[0])
    gate1, up1 = move_core(gate0), move_core(up0)
    own_down = to_group(w_down[0])
    down0, theirs = call(columns_kernel, [shape(half_ff, 2 * quarter)] * 2)(me, own_down)
    down1 = move_core(down0)
    down2 = move_x(theirs, 1)
    down3 = move_core(down2)

    total = None
    for chunk in range(chunks):
        sent = outgoing[chunk].reshape(chips, 2 * SLOTS, quarter)
        incoming = lax.all_to_all(sent, ("y", "z"), split_axis=0, concat_axis=0, tiled=True)
        own = incoming[:, :SLOTS].reshape(at, quarter)
        other = incoming[:, SLOTS:].reshape(at, quarter)
        near, far, across = move_x(own, 1), move_x(other, 3), move_x(other, 2)
        hidden = call(hidden_kernel, shape(2, at, half_ff), flops=2 * at * 4 * quarter * 4 * half_ff)(
            me, own, near, far, across, gate0, up0, gate1, up1
        )
        beside = move_x(hidden, 1)
        result = call(down_kernel, shape(at, 2 * quarter), flops=2 * at * 4 * half_ff * 2 * quarter)(
            me, hidden, beside, down0, down1, down2, down3
        )
        result = result.reshape(chips, SLOTS, 2 * quarter)
        returned = lax.all_to_all(result, ("y", "z"), split_axis=0, concat_axis=0, tiled=True)
        returned = returned.reshape(at, 2 * quarter)
        if chunk == 0:
            total = call(mix_first_kernel, shape(rows, 2 * quarter, dtype=f32))(me, mixing[0], returned)
        elif chunk < chunks - 1:
            total = call(mix_kernel, shape(rows, 2 * quarter, dtype=f32))(me, total, mixing[chunk], returned)
        else:
            keep, send = call(mix_last_kernel, [shape(rows, quarter, dtype=f32), shape(rows, quarter)])(
                me, total, mixing[chunk], returned
            )
    return (keep + move_x(send, 3).astype(f32)).astype(bf16)


def solution(mesh):
    fine = Mesh(mesh.devices.reshape(4, 8, 2, 4), ("y", "z", "c", "x"))
    expert = ("y", "z", "c")
    placed = (
        P(expert, "x"),
        P(expert, None),
        P(expert, None),
        P(expert, None, "x"),
        P(expert, None, "x"),
        P(expert, "x", None),
    )
    return jax.shard_map(shards, mesh=fine, in_specs=placed, out_specs=P(expert, "x"), check_vma=False)
```

```python
import functools

import jax
import jax.numpy as jnp
import numpy as np
from jax import lax
from jax.experimental import pallas as pl
from jax.experimental.pallas import tpu as pltpu
from jax.sharding import Mesh
from jax.sharding import PartitionSpec as P

SLOTS = 8
CAP = 24
VMEM = pl.BlockSpec(memory_space=pltpu.VMEM)
SMEM = pl.BlockSpec(memory_space=pltpu.SMEM)
LIMIT = 60 * 1024 * 1024


def call(kernel, outs, flops=0, moved=0):
    def run(*args):
        return pl.pallas_call(
            kernel,
            out_shape=outs,
            in_specs=[SMEM] + [VMEM] * (len(args) - 1),
            out_specs=jax.tree.map(lambda _: VMEM, outs),
            compiler_params=pltpu.CompilerParams(vmem_limit_bytes=16 * 1024 * 1024),
            cost_estimate=pl.CostEstimate(flops=flops, bytes_accessed=moved, transcendentals=0),
        )(*args)

    return run


def ranked(x_ref, routes_ref, slots, step, weights_ref=None):
    tokens = routes_ref.shape[1]
    lanes = 64 // step * slots
    swap = x_ref[0] // 2
    rows = lax.broadcasted_iota(jnp.int32, (lanes, tokens), 0)
    named, slot = (rows // slots) * step, rows % slots
    routes = routes_ref[...] ^ swap
    member = jnp.zeros((lanes, tokens), jnp.float32)
    weight = jnp.zeros((lanes, tokens), jnp.float32)
    for k in range(routes.shape[0]):
        hit = routes[k : k + 1, :] == named
        member = jnp.where(hit, 1.0, member)
        if weights_ref is not None:
            weight = jnp.where(hit, weights_ref[k : k + 1, :], weight)
    earlier = lax.broadcasted_iota(jnp.int32, (tokens, tokens), 0)
    later = lax.broadcasted_iota(jnp.int32, (tokens, tokens), 1)
    before = jnp.where(earlier < later, 1.0, 0.0).astype(jnp.bfloat16)
    rank = jnp.dot(member.astype(jnp.bfloat16), before, preferred_element_type=jnp.float32)
    return jnp.where(member > 0.0, rank, -1.0), slot, weight


def head_kernel(x_ref, routes_any, tokens_any, gate, up, down, first, rest, joined, routes_ref, tokens_ref, held, sems):
    count = gate.shape[0]
    small = [pltpu.make_async_copy(routes_any, routes_ref, sems.at[0]), pltpu.make_async_copy(tokens_any, tokens_ref, sems.at[1])]
    rows = [pl.ds(i * count, count) for i in range(3)]
    into = [pltpu.make_async_copy(v, held.at[r], sems.at[2 + i]) for i, (v, r) in enumerate(zip((gate, up, down), rows))]
    back = [pltpu.make_async_copy(held.at[r], joined.at[r], sems.at[5 + i]) for i, r in enumerate(rows)]
    for copy in small + into:
        copy.start()
    for copy in small:
        copy.wait()
    tokens = tokens_ref[...]
    rank, slot, _ = ranked(x_ref, routes_ref, SLOTS, 1)
    for step, (out, place) in enumerate(((first, 0), (first, SLOTS), (rest, 0))):
        pick = jnp.where(rank == (slot + step * SLOTS).astype(jnp.float32), 1.0, 0.0).astype(jnp.bfloat16)
        picked = jnp.dot(pick, tokens, preferred_element_type=jnp.float32).astype(jnp.bfloat16)
        chips, kinds, _, quarter = out.shape
        out[:, :, place : place + SLOTS, :] = picked.reshape(chips, kinds, SLOTS, quarter)
        into[step].wait()
        back[step].start()
    for copy in back:
        copy.wait()


def head(me, routes, tokens, weights):
    chips, (count, width) = 32, weights[0].shape
    anywhere = pl.BlockSpec(memory_space=pl.ANY)
    return pl.pallas_call(
        head_kernel,
        out_shape=[
            jax.ShapeDtypeStruct((chips, 2, CAP - SLOTS, tokens.shape[1]), tokens.dtype),
            jax.ShapeDtypeStruct((chips, 2, SLOTS, tokens.shape[1]), tokens.dtype),
            jax.ShapeDtypeStruct((3 * count, width), tokens.dtype),
        ],
        in_specs=[SMEM] + [anywhere] * 5,
        out_specs=[VMEM, VMEM, anywhere],
        scratch_shapes=[
            pltpu.VMEM(routes.shape, routes.dtype),
            pltpu.VMEM(tokens.shape, tokens.dtype),
            pltpu.VMEM((3 * count, width), tokens.dtype),
            pltpu.SemaphoreType.DMA((8,)),
        ],
        compiler_params=pltpu.CompilerParams(vmem_limit_bytes=LIMIT),
        cost_estimate=pl.CostEstimate(flops=0, bytes_accessed=14_000_000, transcendentals=0),
    )(me, routes, tokens, *weights)


def split_kernel(x_ref, both, own, other):
    own[...] = both[:, 0]
    other[...] = both[:, 1]


def weigh_kernel(x_ref, routes_ref, weights_ref, *outs):
    rank, slot, weight = ranked(x_ref, routes_ref, SLOTS, 2, weights_ref)
    for chunk, out in enumerate(outs):
        out[...] = jnp.where(rank == (slot + chunk * SLOTS).astype(jnp.float32), weight, 0.0)


def along(value, weight):
    return lax.dot_general(value, weight, (((1,), (1,)), ((), ())), preferred_element_type=jnp.float32)


def expert_kernel(chunk, x_ref, *refs):
    sources, keep, send, held, sems = refs[:6], refs[6], refs[7], refs[8:14], refs[14]
    count = sources[4].shape[0] // 3
    rows = [pl.ds(i * count, count) for i in range(3)]
    slots = pl.ds(chunk * SLOTS, SLOTS)
    pieces = [pltpu.make_async_copy(sources[i].at[:, slots, :], held[i], sems.at[i]) for i in range(4)]
    weights = []
    for half in range(2):
        for i in range(3):
            source, place = sources[4 + half].at[rows[i]], held[4 + half].at[rows[i]]
            weights.append(pltpu.make_async_copy(source, place, sems.at[4 + 3 * half + i]))
    for copy in pieces + weights:
        copy.start()
    x = x_ref[0]
    quarter = held[0].shape[2]
    blocks = (x, x ^ 1, x ^ 3, x ^ 2)

    def span(q):
        return pl.ds(pl.multiple_of(q * quarter, quarter), quarter)

    for copy in pieces:
        copy.wait()
    values = [piece[...].reshape(-1, quarter) for piece in held[:4]]
    hidden = []
    for half in range(2):
        gate, up = 0.0, 0.0
        weights[3 * half].wait()
        for value, q in zip(values, blocks):
            gate = gate + along(value, held[4 + half][rows[0], span(q)])
        weights[3 * half + 1].wait()
        for value, q in zip(values, blocks):
            up = up + along(value, held[4 + half][rows[1], span(q)])
        hidden.append((gate / (1.0 + jnp.exp(-gate)) * up).astype(jnp.bfloat16))
    weights[2].wait()
    weights[5].wait()
    for out, places in ((send, (x ^ 1, x ^ 2)), (keep, (x, x ^ 3))):
        for place, q in enumerate(places):
            total = jnp.dot(hidden[0], held[4][rows[2], span(q)], preferred_element_type=jnp.float32)
            total = total + jnp.dot(hidden[1], held[5][rows[2], span(q)], preferred_element_type=jnp.float32)
            out[:, place * quarter : (place + 1) * quarter] = total.astype(jnp.bfloat16)


def expert(me, chunk, pieces, weights):
    chips, _, quarter = pieces[0].shape
    count = chips * SLOTS
    operands = [*pieces, *weights]
    out = jax.ShapeDtypeStruct((count, 2 * quarter), jnp.bfloat16)
    held = [(chips, SLOTS, quarter)] * 4 + [v.shape for v in weights]
    return pl.pallas_call(
        functools.partial(expert_kernel, chunk),
        out_shape=[out, out],
        in_specs=[SMEM] + [pl.BlockSpec(memory_space=pl.ANY)] * len(operands),
        out_specs=[VMEM, VMEM],
        scratch_shapes=[pltpu.VMEM(v, jnp.bfloat16) for v in held] + [pltpu.SemaphoreType.DMA((10,))],
        compiler_params=pltpu.CompilerParams(vmem_limit_bytes=LIMIT),
        cost_estimate=pl.CostEstimate(flops=6 * count * 2048 * 704, bytes_accessed=24_000_000, transcendentals=0),
    )(me, *operands)


def across_rows(weight, value):
    return lax.dot_general(weight, value, (((0,), (0,)), ((), ())), preferred_element_type=jnp.float32)


def mixed(weight, value):
    high = weight.astype(jnp.bfloat16)
    low = (weight - high.astype(jnp.float32)).astype(jnp.bfloat16)
    return across_rows(high, value) + across_rows(low, value)


def mix_first_kernel(x_ref, weight, value, out):
    out[...] = mixed(weight[...], value[...])


def mix_kernel(x_ref, total, weight, value, out):
    out[...] = total[...] + mixed(weight[...], value[...])


def mix_last_kernel(x_ref, total, weight, value, keep, send):
    half = keep.shape[1]
    done = total[...] + mixed(weight[...], value[...])
    keep[...] = done[:, :half]
    send[...] = done[:, half:].astype(jnp.bfloat16)


def move_x(value, flip):
    return lax.ppermute(value, "x", [(i, i ^ flip) for i in range(4)])


def move_core(value):
    return lax.ppermute(value, "c", [(0, 1), (1, 0)])


def to_group(value):
    pairs = []
    for x in range(4):
        for core in range(2):
            stays = (x // 2) == core
            target = (x, 1 - core) if stays else (x ^ 3, core)
            pairs.append((core * 4 + x, target[1] * 4 + target[0]))
    return lax.ppermute(value, ("c", "x"), pairs)


def shards(tokens, routes, route_weights, w_gate, w_up, w_down):
    rows, quarter = tokens.shape
    routes, route_weights = routes.T, route_weights.T
    w_gate, w_up = jnp.swapaxes(w_gate, 1, 2), jnp.swapaxes(w_up, 1, 2)
    chips = 32
    me = lax.axis_index("x").astype(jnp.int32).reshape(1)
    bf16, f32 = jnp.bfloat16, jnp.float32

    def shape(*dims, dtype=bf16):
        return jax.ShapeDtypeStruct(dims, dtype)

    first, rest, joined = head(me, routes, tokens, (w_gate[0], w_up[0], w_down[0]))
    kept = to_group(joined)
    chunks = CAP // SLOTS
    mixing = call(weigh_kernel, [shape(chips * SLOTS, rows, dtype=f32)] * chunks)(me, routes, route_weights)

    def across_chips(value):
        return lax.all_to_all(value, ("y", "z"), split_axis=0, concat_axis=0, tiled=True)

    def finish(keep, received):
        return (keep.astype(f32) + received.astype(f32)).astype(bf16).reshape(chips, SLOTS, 2 * quarter)

    tie = lax.optimization_barrier
    def split(value):
        part = shape(chips, value.shape[2], quarter)
        return call(split_kernel, [part, part], moved=6_000_000)(me, value)

    own, other = split(across_chips(first))
    pieces = [own, move_x(own, 1), move_x(other, 3), move_x(other, 2)]
    rest, own = tie((rest, own))
    incoming = across_chips(rest)
    incoming, kept, pieces[1], pieces[2] = tie((incoming, kept, pieces[1], pieces[2]))
    swapped = move_core(kept)
    weights = (kept, swapped)
    own, other = split(incoming)
    later = [own, move_x(own, 1), move_x(other, 3), move_x(other, 2)]
    pieces[0], *later = tie((pieces[0], *later))
    keep0, send0 = expert(me, 0, pieces, weights)
    received0 = move_x(send0, 1)
    keep1, send1 = expert(me, 1, pieces, weights)
    keep2, send2 = expert(me, 0, later, weights)
    received0, send1, send2 = tie((received0, send1, send2))
    received1 = move_x(send1, 1)
    received1, send2 = tie((received1, send2))
    received2 = move_x(send2, 1)
    results = [finish(keep0, received0), finish(keep1, received1), finish(keep2, received2)]
    returned = [across_chips(v).reshape(-1, 2 * quarter) for v in results]
    total = call(mix_first_kernel, shape(rows, 2 * quarter, dtype=f32))(me, mixing[0], returned[0])
    total = call(mix_kernel, shape(rows, 2 * quarter, dtype=f32))(me, total, mixing[1], returned[1])
    keep, send = call(mix_last_kernel, [shape(rows, quarter, dtype=f32), shape(rows, quarter)])(
        me, total, mixing[2], returned[2]
    )
    return (keep + move_x(send, 3).astype(f32)).astype(bf16)


def solution(mesh):
    fine = Mesh(mesh.devices.reshape(4, 8, 2, 4), ("y", "z", "c", "x"))
    expert = ("y", "z", "c")
    placed = (
        P(expert, "x"),
        P(expert, None),
        P(expert, None),
        P(expert, None, "x"),
        P(expert, None, "x"),
        P(expert, "x", None),
    )
    return jax.shard_map(shards, mesh=fine, in_specs=placed, out_specs=P(expert, "x"), check_vma=False)
```

```python
import jax
import jax.numpy as jnp
from jax import lax
from jax.experimental import pallas as pl
from jax.experimental.pallas import tpu as pltpu
from jax.sharding import Mesh
from jax.sharding import PartitionSpec as P

SLOTS = 8
CAP = 24
VMEM = pl.BlockSpec(memory_space=pltpu.VMEM)
SMEM = pl.BlockSpec(memory_space=pltpu.SMEM)
LIMIT = 60 * 1024 * 1024


def call(kernel, outs, flops=0, moved=0):
    def run(*args):
        return pl.pallas_call(
            kernel,
            out_shape=outs,
            in_specs=[SMEM] + [VMEM] * (len(args) - 1),
            out_specs=jax.tree.map(lambda _: VMEM, outs),
            compiler_params=pltpu.CompilerParams(vmem_limit_bytes=16 * 1024 * 1024),
            cost_estimate=pl.CostEstimate(flops=flops, bytes_accessed=moved, transcendentals=0),
        )(*args)

    return run


def expert_order():
    x, core = lax.axis_index("x"), lax.axis_index("c")
    return jnp.where(core == 0, x // 2, 1 - ((x + 1) // 2) % 2).astype(jnp.int32)


def ranked(routes_ref, slots, step, weights_ref=None):
    tokens = routes_ref.shape[1]
    lanes = 64 // step * slots
    swap = expert_order()
    rows = lax.broadcasted_iota(jnp.int32, (lanes, tokens), 0)
    named, slot = (rows // slots) * step, rows % slots
    routes = routes_ref[...] ^ swap
    member = jnp.zeros((lanes, tokens), jnp.float32)
    weight = jnp.zeros((lanes, tokens), jnp.float32)
    for k in range(routes.shape[0]):
        hit = routes[k : k + 1, :] == named
        member = jnp.where(hit, 1.0, member)
        if weights_ref is not None:
            weight = jnp.where(hit, weights_ref[k : k + 1, :], weight)
    earlier = lax.broadcasted_iota(jnp.int32, (tokens, tokens), 0)
    later = lax.broadcasted_iota(jnp.int32, (tokens, tokens), 1)
    before = jnp.where(earlier < later, 1.0, 0.0).astype(jnp.bfloat16)
    rank = jnp.dot(member.astype(jnp.bfloat16), before, preferred_element_type=jnp.float32)
    return jnp.where(member > 0.0, rank, -1.0), slot, weight


def head_kernel(routes_any, tokens_any, gate, up, down, out, joined, routes_ref, tokens_ref, held, sems):
    count = gate.shape[0]
    small = [pltpu.make_async_copy(routes_any, routes_ref, sems.at[0]), pltpu.make_async_copy(tokens_any, tokens_ref, sems.at[1])]
    rows = [pl.ds(i * count, count) for i in range(3)]
    into = [pltpu.make_async_copy(v, held.at[r], sems.at[2 + i]) for i, (v, r) in enumerate(zip((gate, up, down), rows))]
    back = [pltpu.make_async_copy(held.at[r], joined.at[r], sems.at[5 + i]) for i, r in enumerate(rows)]
    for copy in small + into:
        copy.start()
    for copy in small:
        copy.wait()
    tokens = tokens_ref[...]
    rank, slot, _ = ranked(routes_ref, SLOTS, 1)
    chips, kinds, _, quarter = out.shape
    for step in range(3):
        pick = jnp.where(rank == (slot + step * SLOTS).astype(jnp.float32), 1.0, 0.0).astype(jnp.bfloat16)
        picked = jnp.dot(pick, tokens, preferred_element_type=jnp.float32).astype(jnp.bfloat16)
        out[:, :, step * SLOTS : (step + 1) * SLOTS, :] = picked.reshape(chips, kinds, SLOTS, quarter)
        into[step].wait()
        back[step].start()
    for copy in back:
        copy.wait()


def head(routes, tokens, weights):
    chips, (count, width) = 32, weights[0].shape
    anywhere = pl.BlockSpec(memory_space=pl.ANY)
    return pl.pallas_call(
        head_kernel,
        out_shape=[
            jax.ShapeDtypeStruct((chips, 2, CAP, tokens.shape[1]), tokens.dtype),
            jax.ShapeDtypeStruct((3 * count, width), tokens.dtype),
        ],
        in_specs=[anywhere] * 5,
        out_specs=[VMEM, anywhere],
        scratch_shapes=[
            pltpu.VMEM(routes.shape, routes.dtype),
            pltpu.VMEM(tokens.shape, tokens.dtype),
            pltpu.VMEM((3 * count, width), tokens.dtype),
            pltpu.SemaphoreType.DMA((8,)),
        ],
        compiler_params=pltpu.CompilerParams(vmem_limit_bytes=LIMIT),
        cost_estimate=pl.CostEstimate(flops=0, bytes_accessed=14_000_000, transcendentals=0),
    )(routes, tokens, *weights)


def split_kernel(x_ref, both, *outs):
    first = 0
    for own, other in (outs[:2], outs[2:]):
        count = own.shape[1]
        own[...] = both[:, 0, first : first + count, :]
        other[...] = both[:, 1, first : first + count, :]
        first += count


def weigh_kernel(x_ref, routes_ref, weights_ref, *outs):
    first = 0
    for out in outs:
        slots = out.shape[0] // 32
        rank, slot, weight = ranked(routes_ref, slots, 2, weights_ref)
        out[...] = jnp.where(rank == (slot + first).astype(jnp.float32), weight, 0.0)
        first += slots


def along(value, weight):
    return lax.dot_general(value, weight, (((1,), (1,)), ((), ())), preferred_element_type=jnp.float32)


def expert_kernel(x_ref, *refs):
    sources, (local, moved, crossed), keep, send, held, sems = refs[:4], refs[4:7], refs[7], refs[8], refs[9:15], refs[15]
    count = local.shape[0] // 3
    rows = [pl.ds(i * count, count) for i in range(3)]
    pieces = [pltpu.make_async_copy(sources[i], held[i], sems.at[i]) for i in range(4)]

    def weight(source, half, i):
        return pltpu.make_async_copy(source.at[rows[i]], held[4 + half].at[rows[i]], sems.at[4 + 3 * half + i])

    for copy in pieces:
        copy.start()
    for half, flag, yes, no in ((0, x_ref[4], local, moved), (1, x_ref[5], moved, crossed)):

        @pl.when(flag == 1)
        def _():
            for i in range(3):
                weight(yes, half, i).start()

        @pl.when(flag == 0)
        def _():
            for i in range(3):
                weight(no, half, i).start()

    weights = [weight(local, half, i) for half in range(2) for i in range(3)]
    quarter = held[0].shape[2]
    x, partner, far, across = (x_ref[i] for i in range(4))
    blocks = (x, partner, far, across)

    def span(q):
        return pl.ds(pl.multiple_of(q * quarter, quarter), quarter)

    for copy in pieces:
        copy.wait()
    values = [piece[...].reshape(-1, quarter) for piece in held[:4]]
    hidden = []
    for half in range(2):
        gate, up = 0.0, 0.0
        weights[3 * half].wait()
        for value, q in zip(values, blocks):
            gate = gate + along(value, held[4 + half][rows[0], span(q)])
        weights[3 * half + 1].wait()
        for value, q in zip(values, blocks):
            up = up + along(value, held[4 + half][rows[1], span(q)])
        hidden.append((gate / (1.0 + jnp.exp(-gate)) * up).astype(jnp.bfloat16))
    weights[2].wait()
    weights[5].wait()
    for out, places in ((send, (partner, across)), (keep, (x, far))):
        for place, q in enumerate(places):
            total = jnp.dot(hidden[0], held[4][rows[2], span(q)], preferred_element_type=jnp.float32)
            total = total + jnp.dot(hidden[1], held[5][rows[2], span(q)], preferred_element_type=jnp.float32)
            out[:, place * quarter : (place + 1) * quarter] = total.astype(jnp.bfloat16)


def expert(me, slots, pieces, weights):
    chips, _, quarter = pieces[0].shape
    count = chips * slots
    operands = [*pieces, *weights]
    out = jax.ShapeDtypeStruct((count, 2 * quarter), jnp.bfloat16)
    held = [(chips, slots, quarter)] * 4 + [weights[0].shape] * 2
    return pl.pallas_call(
        expert_kernel,
        out_shape=[out, out],
        in_specs=[SMEM] + [pl.BlockSpec(memory_space=pl.ANY)] * len(operands),
        out_specs=[VMEM, VMEM],
        scratch_shapes=[pltpu.VMEM(v, jnp.bfloat16) for v in held] + [pltpu.SemaphoreType.DMA((10,))],
        compiler_params=pltpu.CompilerParams(vmem_limit_bytes=LIMIT),
        cost_estimate=pl.CostEstimate(flops=6 * count * 2048 * 704, bytes_accessed=24_000_000, transcendentals=0),
    )(me, *operands)


def across_rows(weight, value):
    return lax.dot_general(weight, value, (((0,), (0,)), ((), ())), preferred_element_type=jnp.float32)


def mixed(weight, value):
    high = weight.astype(jnp.bfloat16)
    low = (weight - high.astype(jnp.float32)).astype(jnp.bfloat16)
    return across_rows(high, value) + across_rows(low, value)


def mix_first_kernel(x_ref, weight, value, out):
    out[...] = mixed(weight[...], value[...])


def mix_last_kernel(x_ref, total, weight, value, keep, send):
    half = keep.shape[1]
    done = total[...] + mixed(weight[...], value[...])
    keep[...] = done[:, :half]
    send[...] = done[:, half:].astype(jnp.bfloat16)


def move(value, target):
    pairs = []
    for core in range(2):
        for x in range(4):
            place = target(x, core)
            if place is not None:
                pairs.append((core * 4 + x, place[1] * 4 + place[0]))
    return lax.ppermute(value, ("c", "x"), pairs)


def partner_of(x, core):
    return (x ^ (3 if core else 1), core)


def far_of(x, core):
    return (x ^ (1 if core else 3), core)


MOVES = (
    {(2, 1): (2, 0), (3, 1): (3, 0), (1, 0): (1, 1), (2, 0): (2, 1), (1, 1): (0, 1), (3, 0): (0, 0)},
    {(3, 0): (2, 1), (2, 0): (1, 0), (1, 1): (2, 0), (0, 1): (3, 0), (0, 0): (1, 1), (2, 1): (3, 1)},
)


def shards(tokens, routes, route_weights, w_gate, w_up, w_down):
    rows, quarter = tokens.shape
    routes, route_weights = routes.T, route_weights.T
    w_gate, w_up = jnp.swapaxes(w_gate, 1, 2), jnp.swapaxes(w_up, 1, 2)
    chips = 32
    x, core = lax.axis_index("x").astype(jnp.int32), lax.axis_index("c").astype(jnp.int32)
    partner, far = x ^ (1 + 2 * core), x ^ (3 - 2 * core)
    local = (x == 0) | ((x == 1) & (core == 0)) | ((x == 3) & (core == 1))
    me = jnp.stack([x, partner, far, x ^ 2, local.astype(jnp.int32), (x == 0).astype(jnp.int32)])
    bf16, f32 = jnp.bfloat16, jnp.float32

    def shape(*dims, dtype=bf16):
        return jax.ShapeDtypeStruct(dims, dtype)

    outgoing, joined = head(routes, tokens, (w_gate[0], w_up[0], w_down[0]))
    moved, crossed = (move(joined, lambda x, core, m=m: m.get((x, core))) for m in MOVES)
    halves = [shape(chips * n, rows, dtype=f32) for n in (SLOTS, CAP - SLOTS)]
    mixing = call(weigh_kernel, halves)(me, routes, route_weights)

    def across_chips(value):
        return lax.all_to_all(value, ("y", "z"), split_axis=0, concat_axis=0, tiled=True)

    def finish(keep, received):
        return (keep.astype(f32) + received.astype(f32)).astype(bf16).reshape(chips, -1, 2 * quarter)

    tie = lax.optimization_barrier
    incoming, moved, crossed = tie((across_chips(outgoing), moved, crossed))
    weights = (joined, moved, crossed)
    halves = [shape(chips, n, quarter) for n in (SLOTS, CAP - SLOTS) for _ in range(2)]
    own, other, rest_own, rest_other = call(split_kernel, halves, moved=6_000_000)(me, incoming)
    own, far, rest_other = tie((own, move(other, far_of), rest_other))
    near, across, rest_far = move(own, partner_of), move(far, partner_of), move(rest_other, far_of)
    near, across, rest_far, rest_own = tie((near, across, rest_far, rest_own))
    keep0, send0 = expert(me, SLOTS, [own, near, far, across], weights)
    early = across_chips(finish(keep0, move(send0, partner_of)))
    rest = [rest_own, move(rest_own, partner_of), rest_far, move(rest_far, partner_of)]
    keep1, send1 = expert(me, CAP - SLOTS, rest, weights)
    late = finish(keep1, move(send1, partner_of))
    late, early = tie((late, early))
    late = across_chips(late)
    early, late = early.reshape(-1, 2 * quarter), late.reshape(-1, 2 * quarter)
    total = call(mix_first_kernel, shape(rows, 2 * quarter, dtype=f32))(me, mixing[0], early)
    keep, send = call(mix_last_kernel, [shape(rows, quarter, dtype=f32), shape(rows, quarter)])(
        me, total, mixing[1], late
    )
    return (keep + move(send, far_of).astype(f32)).astype(bf16)


def solution(mesh):
    fine = Mesh(mesh.devices.reshape(4, 8, 2, 4), ("y", "z", "c", "x"))
    expert = ("y", "z", "c")
    placed = (
        P(expert, "x"),
        P(expert, None),
        P(expert, None),
        P(expert, None, "x"),
        P(expert, None, "x"),
        P(expert, "x", None),
    )
    return jax.shard_map(shards, mesh=fine, in_specs=placed, out_specs=P(expert, "x"), check_vma=False)
```

```python
import jax
import jax.numpy as jnp
from jax import lax
from jax.experimental import pallas as pl
from jax.experimental.pallas import tpu as pltpu
from jax.sharding import Mesh
from jax.sharding import PartitionSpec as P

SLOTS = 8
CAP = 24
VMEM = pl.BlockSpec(memory_space=pltpu.VMEM)
SMEM = pl.BlockSpec(memory_space=pltpu.SMEM)
LIMIT = 60 * 1024 * 1024


def call(kernel, outs, flops=0, moved=0):
    def run(*args):
        return pl.pallas_call(
            kernel,
            out_shape=outs,
            in_specs=[SMEM] + [VMEM] * (len(args) - 1),
            out_specs=jax.tree.map(lambda _: VMEM, outs),
            compiler_params=pltpu.CompilerParams(vmem_limit_bytes=16 * 1024 * 1024),
            cost_estimate=pl.CostEstimate(flops=flops, bytes_accessed=moved, transcendentals=0),
        )(*args)

    return run


def expert_order():
    x, core = lax.axis_index("x"), lax.axis_index("c")
    return jnp.where(core == 0, x // 2, 1 - ((x + 1) // 2) % 2).astype(jnp.int32)


def ranked(routes_ref, slots, step, weights_ref=None):
    tokens = routes_ref.shape[1]
    lanes = 64 // step * slots
    swap = expert_order()
    rows = lax.broadcasted_iota(jnp.int32, (lanes, tokens), 0)
    named, slot = (rows // slots) * step, rows % slots
    routes = routes_ref[...] ^ swap
    member = jnp.zeros((lanes, tokens), jnp.float32)
    weight = jnp.zeros((lanes, tokens), jnp.float32)
    for k in range(routes.shape[0]):
        hit = routes[k : k + 1, :] == named
        member = jnp.where(hit, 1.0, member)
        if weights_ref is not None:
            weight = jnp.where(hit, weights_ref[k : k + 1, :], weight)
    earlier = lax.broadcasted_iota(jnp.int32, (tokens, tokens), 0)
    later = lax.broadcasted_iota(jnp.int32, (tokens, tokens), 1)
    before = jnp.where(earlier < later, 1.0, 0.0).astype(jnp.bfloat16)
    rank = jnp.dot(member.astype(jnp.bfloat16), before, preferred_element_type=jnp.float32)
    return jnp.where(member > 0.0, rank, -1.0), slot, weight


def head_kernel(routes_any, tokens_any, gate, up, down, out, joined, routes_ref, tokens_ref, held, sems):
    count = gate.shape[0]
    small = [pltpu.make_async_copy(routes_any, routes_ref, sems.at[0]), pltpu.make_async_copy(tokens_any, tokens_ref, sems.at[1])]
    rows = [pl.ds(i * count, count) for i in range(3)]
    into = [pltpu.make_async_copy(v, held.at[r], sems.at[2 + i]) for i, (v, r) in enumerate(zip((gate, up, down), rows))]
    back = [pltpu.make_async_copy(held.at[r], joined.at[r], sems.at[5 + i]) for i, r in enumerate(rows)]
    for copy in small + into:
        copy.start()
    for copy in small:
        copy.wait()
    tokens = tokens_ref[...]
    rank, slot, _ = ranked(routes_ref, SLOTS, 1)
    chips, kinds, _, quarter = out.shape
    for step in range(3):
        pick = jnp.where(rank == (slot + step * SLOTS).astype(jnp.float32), 1.0, 0.0).astype(jnp.bfloat16)
        picked = jnp.dot(pick, tokens, preferred_element_type=jnp.float32).astype(jnp.bfloat16)
        out[:, :, step * SLOTS : (step + 1) * SLOTS, :] = picked.reshape(chips, kinds, SLOTS, quarter)
        into[step].wait()
        back[step].start()
    for copy in back:
        copy.wait()


def head(routes, tokens, weights):
    chips, (count, width) = 32, weights[0].shape
    anywhere = pl.BlockSpec(memory_space=pl.ANY)
    return pl.pallas_call(
        head_kernel,
        out_shape=[
            jax.ShapeDtypeStruct((chips, 2, CAP, tokens.shape[1]), tokens.dtype),
            jax.ShapeDtypeStruct((3 * count, width), tokens.dtype),
        ],
        in_specs=[anywhere] * 5,
        out_specs=[VMEM, anywhere],
        scratch_shapes=[
            pltpu.VMEM(routes.shape, routes.dtype),
            pltpu.VMEM(tokens.shape, tokens.dtype),
            pltpu.VMEM((3 * count, width), tokens.dtype),
            pltpu.SemaphoreType.DMA((8,)),
        ],
        compiler_params=pltpu.CompilerParams(vmem_limit_bytes=LIMIT),
        cost_estimate=pl.CostEstimate(flops=0, bytes_accessed=14_000_000, transcendentals=0),
    )(routes, tokens, *weights)


def split_kernel(x_ref, both, *outs):
    first = 0
    for own, other in (outs[:2], outs[2:]):
        count = own.shape[1]
        own[...] = both[:, 0, first : first + count, :]
        other[...] = both[:, 1, first : first + count, :]
        first += count


def weigh_kernel(x_ref, routes_ref, weights_ref, *outs):
    first = 0
    for out in outs:
        slots = out.shape[0] // 32
        rank, slot, weight = ranked(routes_ref, slots, 2, weights_ref)
        out[...] = jnp.where(rank == (slot + first).astype(jnp.float32), weight, 0.0)
        first += slots


def along(value, weight):
    return lax.dot_general(value, weight, (((1,), (1,)), ((), ())), preferred_element_type=jnp.float32)


def expert_kernel(x_ref, *refs):
    sources, (local, moved, crossed), keep, send, held, sems = refs[:4], refs[4:7], refs[7], refs[8], refs[9:15], refs[15]
    count = local.shape[0] // 3
    rows = [pl.ds(i * count, count) for i in range(3)]
    pieces = [pltpu.make_async_copy(sources[i], held[i], sems.at[i]) for i in range(4)]

    def weight(source, half, i):
        return pltpu.make_async_copy(source.at[rows[i]], held[4 + half].at[rows[i]], sems.at[4 + 3 * half + i])

    for copy in pieces:
        copy.start()
    for half, flag, yes, no in ((0, x_ref[4], local, moved), (1, x_ref[5], moved, crossed)):

        @pl.when(flag == 1)
        def _():
            for i in range(3):
                weight(yes, half, i).start()

        @pl.when(flag == 0)
        def _():
            for i in range(3):
                weight(no, half, i).start()

    weights = [weight(local, half, i) for half in range(2) for i in range(3)]
    quarter = held[0].shape[2]
    x, partner, far, across = (x_ref[i] for i in range(4))
    blocks = (x, partner, far, across)

    def span(q):
        return pl.ds(pl.multiple_of(q * quarter, quarter), quarter)

    for copy in pieces:
        copy.wait()
    values = [piece[...].reshape(-1, quarter) for piece in held[:4]]
    hidden = []
    for half in range(2):
        gate, up = 0.0, 0.0
        weights[3 * half].wait()
        for value, q in zip(values, blocks):
            gate = gate + along(value, held[4 + half][rows[0], span(q)])
        weights[3 * half + 1].wait()
        for value, q in zip(values, blocks):
            up = up + along(value, held[4 + half][rows[1], span(q)])
        hidden.append((gate / (1.0 + jnp.exp(-gate)) * up).astype(jnp.bfloat16))
    weights[2].wait()
    weights[5].wait()
    for out, places in ((send, (partner, across)), (keep, (x, far))):
        for place, q in enumerate(places):
            total = jnp.dot(hidden[0], held[4][rows[2], span(q)], preferred_element_type=jnp.float32)
            total = total + jnp.dot(hidden[1], held[5][rows[2], span(q)], preferred_element_type=jnp.float32)
            out[:, place * quarter : (place + 1) * quarter] = total.astype(jnp.bfloat16)


def expert(me, slots, pieces, weights):
    chips, _, quarter = pieces[0].shape
    count = chips * slots
    operands = [*pieces, *weights]
    out = jax.ShapeDtypeStruct((count, 2 * quarter), jnp.bfloat16)
    held = [(chips, slots, quarter)] * 4 + [weights[0].shape] * 2
    return pl.pallas_call(
        expert_kernel,
        out_shape=[out, out],
        in_specs=[SMEM] + [pl.BlockSpec(memory_space=pl.ANY)] * len(operands),
        out_specs=[VMEM, VMEM],
        scratch_shapes=[pltpu.VMEM(v, jnp.bfloat16) for v in held] + [pltpu.SemaphoreType.DMA((10,))],
        compiler_params=pltpu.CompilerParams(vmem_limit_bytes=24 * 1024 * 1024),
        cost_estimate=pl.CostEstimate(flops=6 * count * 2048 * 704, bytes_accessed=24_000_000, transcendentals=0),
    )(me, *operands)


def across_rows(weight, value):
    return lax.dot_general(weight, value, (((0,), (0,)), ((), ())), preferred_element_type=jnp.float32)


def mixed(weight, value):
    high = weight.astype(jnp.bfloat16)
    low = (weight - high.astype(jnp.float32)).astype(jnp.bfloat16)
    return across_rows(high, value) + across_rows(low, value)


def mix_first_kernel(x_ref, weight, value, out):
    out[...] = mixed(weight[...], value[...])


def mix_last_kernel(x_ref, total, weight, value, keep, send):
    half = keep.shape[1]
    done = total[...] + mixed(weight[...], value[...])
    keep[...] = done[:, :half]
    send[...] = done[:, half:].astype(jnp.bfloat16)


def move(value, target):
    pairs = []
    for core in range(2):
        for x in range(4):
            place = target(x, core)
            if place is not None:
                pairs.append((core * 4 + x, place[1] * 4 + place[0]))
    return lax.ppermute(value, ("c", "x"), pairs)


def partner_of(x, core):
    return (x ^ (3 if core else 1), core)


def far_of(x, core):
    return (x ^ (1 if core else 3), core)


MOVES = (
    {(2, 1): (2, 0), (0, 1): (3, 0), (0, 0): (1, 1), (2, 0): (2, 1), (1, 1): (0, 1), (3, 0): (0, 0)},
    {(3, 0): (2, 1), (2, 0): (1, 0), (1, 1): (2, 0), (3, 1): (3, 0), (1, 0): (1, 1), (2, 1): (3, 1),
     (0, 0): (0, 1), (0, 1): (0, 0)},
)


def shards(tokens, routes, route_weights, w_gate, w_up, w_down):
    rows, quarter = tokens.shape
    routes, route_weights = routes.T, route_weights.T
    w_gate, w_up = jnp.swapaxes(w_gate, 1, 2), jnp.swapaxes(w_up, 1, 2)
    chips = 32
    x, core = lax.axis_index("x").astype(jnp.int32), lax.axis_index("c").astype(jnp.int32)
    partner, far = x ^ (1 + 2 * core), x ^ (3 - 2 * core)
    local = (x == 0) | ((x == 1) & (core == 0)) | ((x == 3) & (core == 1))
    me = jnp.stack([x, partner, far, x ^ 2, local.astype(jnp.int32), (x == 0).astype(jnp.int32)])
    bf16, f32 = jnp.bfloat16, jnp.float32

    def shape(*dims, dtype=bf16):
        return jax.ShapeDtypeStruct(dims, dtype)

    outgoing, joined = head(routes, tokens, (w_gate[0], w_up[0], w_down[0]))
    moved, crossed = (move(joined, lambda x, core, m=m: m.get((x, core))) for m in MOVES)
    halves = [shape(chips * n, rows, dtype=f32) for n in (SLOTS, CAP - SLOTS)]
    mixing = call(weigh_kernel, halves)(me, routes, route_weights)

    def across_chips(value):
        return lax.all_to_all(value, ("y", "z"), split_axis=0, concat_axis=0, tiled=True)

    def finish(keep, received):
        return (keep.astype(f32) + received.astype(f32)).astype(bf16).reshape(chips, -1, 2 * quarter)

    tie = lax.optimization_barrier
    incoming, moved, crossed = tie((across_chips(outgoing), moved, crossed))
    weights = (joined, moved, crossed)
    halves = [shape(chips, n, quarter) for n in (SLOTS, CAP - SLOTS) for _ in range(2)]
    own, other, rest_own, rest_other = call(split_kernel, halves, moved=6_000_000)(me, incoming)
    own, far, rest_other = tie((own, move(other, far_of), rest_other))
    near, across, rest_far = move(own, partner_of), move(far, partner_of), move(rest_other, far_of)
    near, across, rest_far, rest_own = tie((near, across, rest_far, rest_own))
    keep0, send0 = expert(me, SLOTS, [own, near, far, across], weights)
    early = across_chips(finish(keep0, move(send0, partner_of)))
    rest = [rest_own, move(rest_own, partner_of), rest_far, move(rest_far, partner_of)]
    keep1, send1 = expert(me, CAP - SLOTS, rest, weights)
    late = finish(keep1, move(send1, partner_of))
    late, early = tie((late, early))
    late = across_chips(late)
    early, late = early.reshape(-1, 2 * quarter), late.reshape(-1, 2 * quarter)
    total = call(mix_first_kernel, shape(rows, 2 * quarter, dtype=f32))(me, mixing[0], early)
    keep, send = call(mix_last_kernel, [shape(rows, quarter, dtype=f32), shape(rows, quarter)])(
        me, total, mixing[1], late
    )
    return (keep + move(send, far_of).astype(f32)).astype(bf16)


def solution(mesh):
    fine = Mesh(mesh.devices.reshape(4, 8, 2, 4), ("y", "z", "c", "x"))
    expert = ("y", "z", "c")
    placed = (
        P(expert, "x"),
        P(expert, None),
        P(expert, None),
        P(expert, None, "x"),
        P(expert, None, "x"),
        P(expert, "x", None),
    )
    return jax.shard_map(shards, mesh=fine, in_specs=placed, out_specs=P(expert, "x"), check_vma=False)
```

```python
import jax
import jax.numpy as jnp
from jax import lax
from jax.experimental import pallas as pl
from jax.experimental.pallas import tpu as pltpu
from jax.sharding import Mesh
from jax.sharding import PartitionSpec as P

SLOTS = 8
CAP = 24
VMEM = pl.BlockSpec(memory_space=pltpu.VMEM)
SMEM = pl.BlockSpec(memory_space=pltpu.SMEM)
LIMIT = 60 * 1024 * 1024


def call(kernel, outs, flops=0, moved=0):
    def run(*args):
        return pl.pallas_call(
            kernel,
            out_shape=outs,
            in_specs=[SMEM] + [VMEM] * (len(args) - 1),
            out_specs=jax.tree.map(lambda _: VMEM, outs),
            compiler_params=pltpu.CompilerParams(vmem_limit_bytes=16 * 1024 * 1024),
            cost_estimate=pl.CostEstimate(flops=flops, bytes_accessed=moved, transcendentals=0),
        )(*args)

    return run


def expert_order():
    x, core = lax.axis_index("x"), lax.axis_index("c")
    return jnp.where(core == 0, x // 2, 1 - ((x + 1) // 2) % 2).astype(jnp.int32)


def ranked(routes_ref, slots, step, weights_ref=None):
    tokens = routes_ref.shape[1]
    lanes = 64 // step * slots
    swap = expert_order()
    rows = lax.broadcasted_iota(jnp.int32, (lanes, tokens), 0)
    named, slot = (rows // slots) * step, rows % slots
    routes = routes_ref[...] ^ swap
    member = jnp.zeros((lanes, tokens), jnp.float32)
    weight = jnp.zeros((lanes, tokens), jnp.float32)
    for k in range(routes.shape[0]):
        hit = routes[k : k + 1, :] == named
        member = jnp.where(hit, 1.0, member)
        if weights_ref is not None:
            weight = jnp.where(hit, weights_ref[k : k + 1, :], weight)
    earlier = lax.broadcasted_iota(jnp.int32, (tokens, tokens), 0)
    later = lax.broadcasted_iota(jnp.int32, (tokens, tokens), 1)
    before = jnp.where(earlier < later, 1.0, 0.0).astype(jnp.bfloat16)
    rank = jnp.dot(member.astype(jnp.bfloat16), before, preferred_element_type=jnp.float32)
    return jnp.where(member > 0.0, rank, -1.0), slot, weight


def head_kernel(routes_any, tokens_any, gate, up, down, out, joined, routes_ref, tokens_ref, held, sems):
    count = gate.shape[0]
    small = [pltpu.make_async_copy(routes_any, routes_ref, sems.at[0]), pltpu.make_async_copy(tokens_any, tokens_ref, sems.at[1])]
    rows = [pl.ds(i * count, count) for i in range(3)]
    into = [pltpu.make_async_copy(v, held.at[r], sems.at[2 + i]) for i, (v, r) in enumerate(zip((gate, up, down), rows))]
    back = [pltpu.make_async_copy(held.at[r], joined.at[r], sems.at[5 + i]) for i, r in enumerate(rows)]
    for copy in small + into:
        copy.start()
    for copy in small:
        copy.wait()
    tokens = tokens_ref[...]
    rank, slot, _ = ranked(routes_ref, SLOTS, 1)
    for arrived, onward in zip(into, back):
        arrived.wait()
        onward.start()
    chips, kinds, _, quarter = out.shape
    for step in range(3):
        pick = jnp.where(rank == (slot + step * SLOTS).astype(jnp.float32), 1.0, 0.0).astype(jnp.bfloat16)
        picked = jnp.dot(pick, tokens, preferred_element_type=jnp.float32).astype(jnp.bfloat16)
        out[:, :, step * SLOTS : (step + 1) * SLOTS, :] = picked.reshape(chips, kinds, SLOTS, quarter)
    for copy in back:
        copy.wait()


def head(routes, tokens, weights):
    chips, (count, width) = 32, weights[0].shape
    anywhere = pl.BlockSpec(memory_space=pl.ANY)
    return pl.pallas_call(
        head_kernel,
        out_shape=[
            jax.ShapeDtypeStruct((chips, 2, CAP, tokens.shape[1]), tokens.dtype),
            jax.ShapeDtypeStruct((3 * count, width), tokens.dtype),
        ],
        in_specs=[anywhere] * 5,
        out_specs=[VMEM, anywhere],
        scratch_shapes=[
            pltpu.VMEM(routes.shape, routes.dtype),
            pltpu.VMEM(tokens.shape, tokens.dtype),
            pltpu.VMEM((3 * count, width), tokens.dtype),
            pltpu.SemaphoreType.DMA((8,)),
        ],
        compiler_params=pltpu.CompilerParams(vmem_limit_bytes=LIMIT),
        cost_estimate=pl.CostEstimate(flops=0, bytes_accessed=14_000_000, transcendentals=0),
    )(routes, tokens, *weights)


def split_kernel(x_ref, both, *outs):
    first = 0
    for own, other in (outs[:2], outs[2:]):
        count = own.shape[1]
        own[...] = both[:, 0, first : first + count, :]
        other[...] = both[:, 1, first : first + count, :]
        first += count


def weigh_kernel(x_ref, routes_ref, weights_ref, *outs):
    first = 0
    for out in outs:
        slots = out.shape[0] // 32
        rank, slot, weight = ranked(routes_ref, slots, 2, weights_ref)
        out[...] = jnp.where(rank == (slot + first).astype(jnp.float32), weight, 0.0)
        first += slots


def along(value, weight):
    return lax.dot_general(value, weight, (((1,), (1,)), ((), ())), preferred_element_type=jnp.float32)


def expert_kernel(x_ref, *refs):
    sources, (local, moved, crossed), keep, send, held, sems = refs[:4], refs[4:7], refs[7], refs[8], refs[9:15], refs[15]
    count = local.shape[0] // 3
    rows = [pl.ds(i * count, count) for i in range(3)]
    pieces = [pltpu.make_async_copy(sources[i], held[i], sems.at[i]) for i in range(4)]

    def weight(source, half, i):
        return pltpu.make_async_copy(source.at[rows[i]], held[4 + half].at[rows[i]], sems.at[4 + 3 * half + i])

    for copy in pieces:
        copy.start()
    for half, flag, yes, no in ((0, x_ref[4], local, moved), (1, x_ref[5], moved, crossed)):

        @pl.when(flag == 1)
        def _():
            for i in range(3):
                weight(yes, half, i).start()

        @pl.when(flag == 0)
        def _():
            for i in range(3):
                weight(no, half, i).start()

    weights = [weight(local, half, i) for half in range(2) for i in range(3)]
    quarter = held[0].shape[2]
    x, partner, far, across = (x_ref[i] for i in range(4))
    blocks = (x, partner, far, across)

    def span(q):
        return pl.ds(pl.multiple_of(q * quarter, quarter), quarter)

    for copy in pieces:
        copy.wait()
    values = [piece[...].reshape(-1, quarter) for piece in held[:4]]
    hidden = []
    for half in range(2):
        gate, up = 0.0, 0.0
        weights[3 * half].wait()
        for value, q in zip(values, blocks):
            gate = gate + along(value, held[4 + half][rows[0], span(q)])
        weights[3 * half + 1].wait()
        for value, q in zip(values, blocks):
            up = up + along(value, held[4 + half][rows[1], span(q)])
        hidden.append((gate / (1.0 + jnp.exp(-gate)) * up).astype(jnp.bfloat16))
    weights[2].wait()
    weights[5].wait()
    for out, places in ((send, (partner, across)), (keep, (x, far))):
        for place, q in enumerate(places):
            total = jnp.dot(hidden[0], held[4][rows[2], span(q)], preferred_element_type=jnp.float32)
            total = total + jnp.dot(hidden[1], held[5][rows[2], span(q)], preferred_element_type=jnp.float32)
            out[:, place * quarter : (place + 1) * quarter] = total.astype(jnp.bfloat16)


def expert(me, slots, pieces, weights):
    chips, _, quarter = pieces[0].shape
    count = chips * slots
    operands = [*pieces, *weights]
    out = jax.ShapeDtypeStruct((count, 2 * quarter), jnp.bfloat16)
    held = [(chips, slots, quarter)] * 4 + [weights[0].shape] * 2
    return pl.pallas_call(
        expert_kernel,
        out_shape=[out, out],
        in_specs=[SMEM] + [pl.BlockSpec(memory_space=pl.ANY)] * len(operands),
        out_specs=[VMEM, VMEM],
        scratch_shapes=[pltpu.VMEM(v, jnp.bfloat16) for v in held] + [pltpu.SemaphoreType.DMA((10,))],
        compiler_params=pltpu.CompilerParams(vmem_limit_bytes=24 * 1024 * 1024),
        cost_estimate=pl.CostEstimate(flops=6 * count * 2048 * 704, bytes_accessed=24_000_000, transcendentals=0),
    )(me, *operands)


def across_rows(weight, value):
    return lax.dot_general(weight, value, (((0,), (0,)), ((), ())), preferred_element_type=jnp.float32)


def mixed(weight, value):
    high = weight.astype(jnp.bfloat16)
    low = (weight - high.astype(jnp.float32)).astype(jnp.bfloat16)
    return across_rows(high, value) + across_rows(low, value)


def mix_first_kernel(x_ref, weight, value, out):
    out[...] = mixed(weight[...], value[...])


def mix_last_kernel(x_ref, total, weight, value, keep, send):
    half = keep.shape[1]
    done = total[...] + mixed(weight[...], value[...])
    keep[...] = done[:, :half]
    send[...] = done[:, half:].astype(jnp.bfloat16)


def move(value, target):
    pairs = []
    for core in range(2):
        for x in range(4):
            place = target(x, core)
            if place is not None:
                pairs.append((core * 4 + x, place[1] * 4 + place[0]))
    return lax.ppermute(value, ("c", "x"), pairs)


def partner_of(x, core):
    return (x ^ (3 if core else 1), core)


def far_of(x, core):
    return (x ^ (1 if core else 3), core)


MOVES = (
    {(2, 1): (2, 0), (0, 1): (3, 0), (0, 0): (1, 1), (2, 0): (2, 1), (1, 1): (0, 1), (3, 0): (0, 0)},
    {(3, 0): (2, 1), (2, 0): (1, 0), (1, 1): (2, 0), (3, 1): (3, 0), (1, 0): (1, 1), (2, 1): (3, 1),
     (0, 0): (0, 1), (0, 1): (0, 0)},
)


def shards(tokens, routes, route_weights, w_gate, w_up, w_down):
    rows, quarter = tokens.shape
    routes, route_weights = routes.T, route_weights.T
    w_gate, w_up = jnp.swapaxes(w_gate, 1, 2), jnp.swapaxes(w_up, 1, 2)
    chips = 32
    x, core = lax.axis_index("x").astype(jnp.int32), lax.axis_index("c").astype(jnp.int32)
    partner, far = x ^ (1 + 2 * core), x ^ (3 - 2 * core)
    local = (x == 0) | ((x == 1) & (core == 0)) | ((x == 3) & (core == 1))
    me = jnp.stack([x, partner, far, x ^ 2, local.astype(jnp.int32), (x == 0).astype(jnp.int32)])
    bf16, f32 = jnp.bfloat16, jnp.float32

    def shape(*dims, dtype=bf16):
        return jax.ShapeDtypeStruct(dims, dtype)

    outgoing, joined = head(routes, tokens, (w_gate[0], w_up[0], w_down[0]))
    moved, crossed = (move(joined, lambda x, core, m=m: m.get((x, core))) for m in MOVES)
    halves = [shape(chips * n, rows, dtype=f32) for n in (SLOTS, CAP - SLOTS)]
    mixing = call(weigh_kernel, halves)(me, routes, route_weights)

    def across_chips(value):
        return lax.all_to_all(value, ("y", "z"), split_axis=0, concat_axis=0, tiled=True)

    def finish(keep, received):
        return (keep.astype(f32) + received.astype(f32)).astype(bf16).reshape(chips, -1, 2 * quarter)

    tie = lax.optimization_barrier
    incoming, moved, crossed = tie((across_chips(outgoing), moved, crossed))
    weights = (joined, moved, crossed)
    halves = [shape(chips, n, quarter) for n in (SLOTS, CAP - SLOTS) for _ in range(2)]
    own, other, rest_own, rest_other = call(split_kernel, halves, moved=6_000_000)(me, incoming)
    own, far, rest_other = tie((own, move(other, far_of), rest_other))
    near, across, rest_far = move(own, partner_of), move(far, partner_of), move(rest_other, far_of)
    near, across, rest_far, rest_own = tie((near, across, rest_far, rest_own))
    keep0, send0 = expert(me, SLOTS, [own, near, far, across], weights)
    early = across_chips(finish(keep0, move(send0, partner_of)))
    rest = [rest_own, move(rest_own, partner_of), rest_far, move(rest_far, partner_of)]
    keep1, send1 = expert(me, CAP - SLOTS, rest, weights)
    late = finish(keep1, move(send1, partner_of))
    late, early = tie((late, early))
    late = across_chips(late)
    early, late = early.reshape(-1, 2 * quarter), late.reshape(-1, 2 * quarter)
    total = call(mix_first_kernel, shape(rows, 2 * quarter, dtype=f32))(me, mixing[0], early)
    keep, send = call(mix_last_kernel, [shape(rows, quarter, dtype=f32), shape(rows, quarter)])(
        me, total, mixing[1], late
    )
    return (keep + move(send, far_of).astype(f32)).astype(bf16)


def solution(mesh):
    fine = Mesh(mesh.devices.reshape(4, 8, 2, 4), ("y", "z", "c", "x"))
    expert = ("y", "z", "c")
    placed = (
        P(expert, "x"),
        P(expert, None),
        P(expert, None),
        P(expert, None, "x"),
        P(expert, None, "x"),
        P(expert, "x", None),
    )
    return jax.shard_map(shards, mesh=fine, in_specs=placed, out_specs=P(expert, "x"), check_vma=False)
```
